256 devices in a mesh: grp: 8 (over z), seq: 32 (over x, y, core).
Axes of the slice: x: 4, y: 4, z: 8, core: 2. Of those that a mesh axis runs over, the one named last changes fastest.
Arguments:
- queries: bfloat16 [8, 1024, 4096], P('grp', 'seq'), may hold values from -96 to 96
- attn_keys: bfloat16 [8, 1024, 4096], P('grp', 'seq'), may hold values from -4 to 4
- attn_values: bfloat16 [8, 1024, 4096], P('grp', 'seq'), may hold values from -6 to 6
- byte_grads: bfloat16 [8, 8192, 4096], P('grp', 'seq'), may hold values from -6 to 6
- seg_starts: int32 [8, 32, 32], P('grp', 'seq'), may hold values from 0 to 256, as said below
- up_gain: float32 [4096], replicated, may hold values from 0.1 to 1.9
Outputs:
- grad_queries: bfloat16 [8, 1024, 4096], P('grp', 'seq')
- grad_keys: bfloat16 [8, 1024, 4096], P('grp', 'seq')
- grad_values: bfloat16 [8, 1024, 4096], P('grp', 'seq')
- grad_gain: float32 [4096], P('seq')
The draws below stay inside these ranges and needn't reach their ends.
Inputs may be any that keep to these rules, and one draw needn't show every extreme that they name: `seg_starts`: in every row each shard's entries rise strictly, the used ones below 256 and the unused slots after them equal to 256; every shard starts at least 8 segments and some shard of every row exactly 32; shard 0's first entry is 0.
All inputs are finite; a program needn't handle non-finite values.
Results may differ from the reference program's by a relative error of at most 0.012.
Values may be sent and summed in bfloat16 or wider, within the bound.
No kernel may reach another device: no remote copies, remote signals or barrier semaphores. Data moves between devices by JAX's collectives and lax.ppermute only.
A program may use at most 64 MiB of HBM per device.

```python
import math
import jax
import jax.numpy as jnp
from jax import lax

D = 4096
HEADS = 32
HD = 128
BYTE_DEV = 256
CAP = 32
ROWS = 8
BYTES = 8192
S_PAD = 1024
N_SEQ = 32


def drawn_rows(key):
    full_shape = (ROWS, S_PAD, D)
    key_base = jnp.clip(jax.random.normal(jax.random.fold_in(key, 11), full_shape, jnp.float32), -4.0, 4.0)
    query_base = jnp.clip(jax.random.normal(jax.random.fold_in(key, 12), full_shape, jnp.float32), -4.0, 4.0)
    return (query_base, key_base)


def draw_queries(key, part):
    return drawn_rows(key)[0].astype(jnp.bfloat16)


def draw_attn_keys(key, part):
    return drawn_rows(key)[1].astype(jnp.bfloat16)


def draw_seg_starts(key, part):
    counts = jax.random.randint(jax.random.fold_in(key, 21), (ROWS, N_SEQ), CAP // 4, CAP + 1)
    chosen_full = jax.random.randint(jax.random.fold_in(key, 22), (ROWS, 1), 0, N_SEQ)
    counts = jnp.where(jnp.arange(N_SEQ)[None, :] == chosen_full, CAP, counts)
    perm_keys = jax.random.split(jax.random.fold_in(key, 23), ROWS * N_SEQ)
    orders = jax.vmap(lambda single_key: jax.random.permutation(single_key, BYTE_DEV))(perm_keys)
    orders = orders.reshape(ROWS, N_SEQ, BYTE_DEV).astype(jnp.int32)
    leader = orders[:, :, :1]
    swapped = jnp.where(orders == 0, leader, orders)
    swapped = swapped.at[:, :, 0].set(0)
    shard_zero = (jnp.arange(N_SEQ) == 0)[None, :, None]
    orders = jnp.where(shard_zero, swapped, orders)
    chosen = orders[:, :, :CAP]
    in_use = jnp.arange(CAP)[None, None, :] < counts[:, :, None]
    chosen = jnp.where(in_use, chosen, BYTE_DEV)
    return jnp.sort(chosen, axis=-1).astype(jnp.int32)


def with_spikes(values, own_key, source, target, blocks, factor):
    owner, partner = [(jnp.arange(values.shape[dim]) // (values.shape[dim] // blocks)).reshape([-1 if axis == dim else 1 for axis in range(values.ndim)]) for dim in (source, target)]
    chosen = jax.random.permutation(own_key, blocks)[partner]
    strong = (owner == chosen) | (owner == (partner + blocks // 2) % blocks)
    return jnp.where(strong, factor * values, values)


def shard_levels(key, dims, cuts, low, largest):
    factor_of, own = 1.0, jax.random.fold_in(key, 6)
    for axis_at, parts in cuts:
        heights = jnp.exp(jax.random.uniform(jax.random.fold_in(own, axis_at), (parts,), jnp.float32, low / len(cuts), largest / len(cuts)))
        factor_of = factor_of * jnp.repeat(heights, dims[axis_at] // parts).reshape([-1 if axis == axis_at else 1 for axis in range(len(dims))])
    return factor_of


def centred(own_key, extent, scale, bound, pieces=(), kind=jnp.bfloat16):
    array = jax.random.normal(own_key, extent, jnp.float32) * scale
    if len(pieces) > 0:
        array = shard_levels(own_key, extent, pieces, -0.22, 0.18) * array
    return jnp.clip(array, min=-bound, max=bound).astype(kind)


def bell_draw_with(stream_key, dims, deviation, limit, cuts, heavy, held_as=jnp.bfloat16):
    values = deviation * jax.random.normal(stream_key, dims, jnp.float32)
    if cuts:
        values = values * shard_levels(stream_key, dims, cuts, -0.22, 0.18)
    return jnp.clip(with_spikes(values, jax.random.fold_in(stream_key, 3), *heavy), -limit, limit).astype(held_as)


def setup_inputs(seed: int = 0) -> dict:
    arg_keys = jax.random.split(jax.random.key(seed), 7)
    return {
        "queries": draw_queries(jax.random.fold_in(arg_keys[6], 71), 0),
        "attn_keys": draw_attn_keys(jax.random.fold_in(arg_keys[6], 71), 0),
        "attn_values": centred(arg_keys[2], (ROWS, S_PAD, D), 1.0, 6.0, ((0, 8), (1, 32))),
        "byte_grads": bell_draw_with(arg_keys[3], (ROWS, BYTES, D), 0.5, 6.0, ((0, 8), (1, 32)), (1, 2, 32, 2.75)),
        "seg_starts": draw_seg_starts(jax.random.fold_in(arg_keys[6], 71), 0),
        "up_gain": jnp.clip(1.0 + 0.18 * jax.random.normal(arg_keys[5], (D,), jnp.float32), 0.1, 1.9),
    }


def head_backward(query_head, key_head, value_head, upstream, key_valid):
    seq_rows = query_head.shape[0]
    scaling = 1.0 / math.sqrt(HD)
    scores = jnp.dot(query_head, key_head.T, preferred_element_type=jnp.float32) * scaling
    row_ids = jnp.arange(seq_rows, dtype=jnp.int32)[:, None]
    col_ids = jnp.arange(seq_rows, dtype=jnp.int32)[None, :]
    allowed = (col_ids <= row_ids) & key_valid[None, :]
    scores = jnp.where(allowed, scores, -1e+30)
    row_max = lax.optimization_barrier(jnp.max(scores, axis=1, keepdims=True))
    weights = jnp.exp(scores - row_max)
    attn_probs = weights / lax.optimization_barrier(jnp.sum(weights, axis=1, keepdims=True))
    probs_low = attn_probs.astype(jnp.bfloat16)
    attn_out = jnp.dot(probs_low, value_head, preferred_element_type=jnp.float32).astype(jnp.bfloat16)
    grad_probs = jnp.dot(upstream, value_head.T, preferred_element_type=jnp.float32)
    row_delta = lax.optimization_barrier(jnp.sum(upstream.astype(jnp.float32) * attn_out.astype(jnp.float32), axis=1, keepdims=True))
    grad_scores = (attn_probs * (grad_probs - row_delta)).astype(jnp.bfloat16)
    grad_query = (jnp.dot(grad_scores, key_head, preferred_element_type=jnp.float32) * scaling).astype(jnp.bfloat16)
    grad_key = (jnp.dot(grad_scores.T, query_head, preferred_element_type=jnp.float32) * scaling).astype(jnp.bfloat16)
    grad_value = jnp.dot(probs_low.T, upstream, preferred_element_type=jnp.float32).astype(jnp.bfloat16)
    return (grad_query, grad_key, grad_value, attn_out)

def reference(queries, attn_keys, attn_values, byte_grads, seg_starts, up_gain):

    def one_row(packed):
        row_queries, row_keys, row_values, row_grads, row_starts = packed
        filled = lax.optimization_barrier(jnp.sum((row_starts < BYTE_DEV).astype(jnp.int32), axis=1))
        position = jnp.arange(BYTE_DEV, dtype=jnp.int32)
        started = lax.optimization_barrier(jnp.sum((row_starts[:, None, :] <= position[None, :, None]).astype(jnp.int32), axis=2))
        shard_ids = jnp.arange(N_SEQ, dtype=jnp.int32)[:, None]
        previous = jnp.roll(filled, 1)[:, None]
        owner_slot = jnp.where(started > 0, shard_ids * CAP + started - 1, (shard_ids - 1) * CAP + previous - 1)
        owner_slot = owner_slot.reshape(-1).astype(jnp.int32)
        pooled = jax.ops.segment_sum(row_grads.astype(jnp.float32), owner_slot, num_segments=S_PAD)
        pooled_low = pooled.astype(jnp.bfloat16)
        upstream = (up_gain[None, :].astype(jnp.float32) * pooled_low.astype(jnp.float32)).astype(jnp.bfloat16)
        key_valid = (row_starts < BYTE_DEV).reshape(-1)

        def split_heads(tensor):
            return tensor.reshape(S_PAD, HEADS, HD).transpose(1, 0, 2)

        def join_heads(tensor):
            return tensor.transpose(1, 0, 2).reshape(S_PAD, D)

        def per_head(head_items):
            return head_backward(head_items[0], head_items[1], head_items[2], head_items[3], key_valid)
        results = lax.map(per_head, (split_heads(row_queries), split_heads(row_keys), split_heads(row_values), split_heads(upstream)))
        grad_query = join_heads(results[0])
        grad_key = join_heads(results[1])
        grad_value = join_heads(results[2])
        attn_out = join_heads(results[3])
        gain_terms = lax.optimization_barrier(jnp.sum(attn_out.astype(jnp.float32) * pooled_low.astype(jnp.float32), axis=0))
        return (grad_query, grad_key, grad_value, gain_terms)
    grad_queries, grad_keys, grad_values, gain_terms = lax.map(one_row, (queries, attn_keys, attn_values, byte_grads, seg_starts))
    return (grad_queries, grad_keys, grad_values, lax.optimization_barrier(jnp.sum(gain_terms, axis=0)))
```

```python
import functools
import math

import jax
import jax.numpy as jnp
from jax import lax
from jax.experimental import pallas as pl
from jax.experimental.pallas import tpu as pltpu
from jax.sharding import PartitionSpec as P

HD = 128
EXTRA = 16


def start_columns(starts, byte_count):
    count = starts.shape[1]
    row = lax.broadcasted_iota(jnp.int32, (count, count), 0)
    col = lax.broadcasted_iota(jnp.int32, (count, count), 1)
    spread = jnp.broadcast_to(starts, (count, count))
    begin = jnp.sum(jnp.where(row == col, spread, 0), axis=1, keepdims=True)
    end = jnp.sum(jnp.where(row + 1 == col, spread, 0), axis=1, keepdims=True)
    last_row = lax.broadcasted_iota(jnp.int32, (count, 1), 0) == count - 1
    return begin, jnp.where(last_row, byte_count, end)


def pack_kernel(query_ref, key_ref, value_ref, bytes_ref, starts_ref, packed_ref):
    heads = packed_ref.shape[0]
    slots = query_ref.shape[1]
    byte_count = bytes_ref.shape[1]
    starts = starts_ref[0].astype(jnp.float32)
    begin, end = start_columns(starts, float(byte_count))
    position = lax.broadcasted_iota(jnp.int32, (slots, byte_count), 1).astype(jnp.float32)
    own = (begin <= position) & (position < end)
    filled = jnp.sum(jnp.where(starts < byte_count, 1.0, 0.0), axis=1, keepdims=True)
    first = jnp.min(starts, axis=1, keepdims=True)
    last = jnp.max(jnp.where(starts < byte_count, starts, -1.0), axis=1, keepdims=True)
    row = lax.broadcasted_iota(jnp.int32, (EXTRA, byte_count), 0)
    place = lax.broadcasted_iota(jnp.int32, (EXTRA, byte_count), 1).astype(jnp.float32)
    leading = (row < 2) & (place < first)
    tail = (row == 2) & (place >= last)
    member = jnp.concatenate(
        [jnp.where(own, 1.0, 0.0), jnp.where(leading | tail, 1.0, 0.0)], axis=0
    ).astype(jnp.bfloat16)
    sums = jnp.dot(member, bytes_ref[0], preferred_element_type=jnp.float32)
    extra = sums[slots:]
    low = extra - extra.astype(jnp.bfloat16).astype(jnp.float32)
    kind = lax.broadcasted_iota(jnp.int32, extra.shape, 0)
    extra = jnp.where(kind == 0, extra, jnp.where(kind == 3, filled, low)).astype(jnp.bfloat16)
    pooled = sums[:slots].astype(jnp.bfloat16)
    for head in range(heads):
        cols = slice(head * HD, (head + 1) * HD)
        packed_ref[head, 0:slots, :] = query_ref[0, :, cols]
        packed_ref[head, slots : 2 * slots, :] = key_ref[0, :, cols]
        packed_ref[head, 2 * slots : 3 * slots, :] = value_ref[0, :, cols]
        packed_ref[head, 3 * slots : 4 * slots, :] = pooled[:, cols]
        packed_ref[head, 4 * slots :, :] = extra[:, cols]


def pack(queries, attn_keys, attn_values, byte_grads, seg_starts, steps):
    slots, width = queries.shape[1:]
    byte_count = byte_grads.shape[1]
    cap = seg_starts.shape[2]
    cols = width // steps
    heads = width // HD
    rows = 4 * slots + EXTRA
    slot_spec = pl.BlockSpec((1, slots, cols), lambda i: (0, 0, i))
    return pl.pallas_call(
        pack_kernel,
        grid=(steps,),
        in_specs=[
            slot_spec,
            slot_spec,
            slot_spec,
            pl.BlockSpec((1, byte_count, cols), lambda i: (0, 0, i)),
            pl.BlockSpec((1, 1, cap), lambda i: (0, 0, 0)),
        ],
        out_specs=pl.BlockSpec((heads // steps, rows, HD), lambda i: (i, 0, 0)),
        out_shape=jax.ShapeDtypeStruct((heads, rows, HD), jnp.bfloat16),
        compiler_params=pltpu.CompilerParams(vmem_limit_bytes=32 * 2**20),
        name="pool_and_pack",
    )(queries, attn_keys, attn_values, byte_grads, seg_starts)


def attention_kernel(
    block, packed_ref, gain_ref, grads_ref, gain_grad_ref, upstream_ref, pooled_ref, bias_ref, dk_ref, dv_ref
):
    shards, rows, width = packed_ref.shape
    slots = (rows - EXTRA) // 4
    total = shards * slots
    scaling = 1.0 / math.sqrt(width)

    extra = packed_ref[:, 4 * slots :, :].astype(jnp.float32)
    carried = extra[:, 0:1, :] + extra[:, 1:2, :]
    incoming = jnp.concatenate([carried[1:], jnp.zeros_like(carried[:1])], axis=0)
    incoming = incoming + extra[:, 2:3, :]
    filled = extra[:, 3:4, :]
    slot = lax.broadcasted_iota(jnp.int32, (shards, slots, width), 1).astype(jnp.float32)
    pooled = packed_ref[:, 3 * slots : 4 * slots, :].astype(jnp.float32)
    pooled = pooled + jnp.where(slot == filled - 1.0, incoming, 0.0)
    pooled = pooled.reshape(total, width).astype(jnp.bfloat16)
    pooled_ref[...] = pooled
    upstream_ref[...] = (gain_ref[...] * pooled.astype(jnp.float32)).astype(jnp.bfloat16)
    bias_ref[...] = jnp.where(slot < filled, 0.0, -1e30).reshape(total, width)

    query = packed_ref[:, 0:slots, :].reshape(total, width)
    key = packed_ref[:, slots : 2 * slots, :].reshape(total, width)
    value = packed_ref[:, 2 * slots : 3 * slots, :].reshape(total, width)
    key_t = key.T
    value_t = value.T
    gain_grad = jnp.zeros((1, width), jnp.float32)
    contract_last = (((1,), (1,)), ((), ()))
    for index in range(total // block):
        first = index * block
        prefix = first + block
        query_block = query[first:prefix]
        upstream_block = upstream_ref[first:prefix]
        scores = lax.dot_general(
            key[:prefix], query_block, contract_last, preferred_element_type=jnp.float32
        )
        bias = jnp.concatenate([bias_ref[:prefix]] * (block // width), axis=1)
        scores = scores + bias
        key_ids = lax.broadcasted_iota(jnp.int32, (block, block), 0)
        query_ids = lax.broadcasted_iota(jnp.int32, (block, block), 1)
        diagonal = jnp.where(key_ids <= query_ids, scores[first:], -1e30)
        scores = jnp.concatenate([scores[:first], diagonal], axis=0) if first else diagonal
        row_max = jnp.max(scores, axis=0, keepdims=True)
        weights = jnp.exp((scores - row_max) * scaling)
        probs = weights * (1.0 / jnp.sum(weights, axis=0, keepdims=True))
        probs_low = probs.astype(jnp.bfloat16)
        out_t = jnp.dot(value_t[:, :prefix], probs_low, preferred_element_type=jnp.float32)
        out_t = out_t.astype(jnp.bfloat16).astype(jnp.float32)
        upstream_t = upstream_block.astype(jnp.float32).T
        row_delta = jnp.sum(upstream_t * out_t, axis=0, keepdims=True)
        gain_grad += jnp.sum(
            out_t.T * pooled_ref[first:prefix].astype(jnp.float32), axis=0, keepdims=True
        )
        grad_probs = lax.dot_general(
            value[:prefix], upstream_block, contract_last, preferred_element_type=jnp.float32
        )
        grad_scores = (probs * (grad_probs - row_delta)).astype(jnp.bfloat16)
        dq_t = jnp.dot(key_t[:, :prefix], grad_scores, preferred_element_type=jnp.float32)
        dq = (dq_t.T * scaling).astype(jnp.bfloat16)
        owners = slice(first // slots, prefix // slots)
        grads_ref[owners, 0:slots, :] = dq.reshape(block // slots, slots, width)
        dk = jnp.dot(grad_scores, query_block, preferred_element_type=jnp.float32)
        dv = jnp.dot(probs_low, upstream_block, preferred_element_type=jnp.float32)
        if first:
            dk_ref[:first] += dk[:first]
            dv_ref[:first] += dv[:first]
        dk_ref[first:prefix] = dk[first:]
        dv_ref[first:prefix] = dv[first:]
    grads_ref[:, slots : 2 * slots, :] = (
        (dk_ref[...] * scaling).astype(jnp.bfloat16).reshape(shards, slots, width)
    )
    grads_ref[:, 2 * slots :, :] = dv_ref[...].astype(jnp.bfloat16).reshape(shards, slots, width)
    gain_grad_ref[...] = gain_grad


def attention(packed, gain, block):
    shards, rows, width = packed.shape
    slots = (rows - EXTRA) // 4
    total = shards * slots
    vmem = pl.BlockSpec(memory_space=pltpu.VMEM)
    return pl.pallas_call(
        functools.partial(attention_kernel, block),
        in_specs=[vmem, vmem],
        out_specs=[vmem, vmem],
        out_shape=[
            jax.ShapeDtypeStruct((shards, 3 * slots, width), jnp.bfloat16),
            jax.ShapeDtypeStruct((1, width), jnp.float32),
        ],
        scratch_shapes=[
            pltpu.VMEM((total, width), jnp.bfloat16),
            pltpu.VMEM((total, width), jnp.bfloat16),
            pltpu.VMEM((total, width), jnp.float32),
            pltpu.VMEM((total, width), jnp.float32),
            pltpu.VMEM((total, width), jnp.float32),
        ],
        compiler_params=pltpu.CompilerParams(vmem_limit_bytes=40 * 2**20),
        name="attention_grads",
    )(packed, gain)


def unpack_kernel(grads_ref, dq_ref, dk_ref, dv_ref):
    slots = dq_ref.shape[1]
    for head in range(grads_ref.shape[0]):
        cols = slice(head * HD, (head + 1) * HD)
        dq_ref[0, :, cols] = grads_ref[head, 0:slots, :]
        dk_ref[0, :, cols] = grads_ref[head, slots : 2 * slots, :]
        dv_ref[0, :, cols] = grads_ref[head, 2 * slots :, :]


def unpack(grads):
    heads, rows, width = grads.shape
    out = jax.ShapeDtypeStruct((1, rows // 3, heads * width), jnp.bfloat16)
    vmem = pl.BlockSpec(memory_space=pltpu.VMEM)
    return pl.pallas_call(
        unpack_kernel,
        in_specs=[vmem],
        out_specs=[vmem] * 3,
        out_shape=[out] * 3,
        compiler_params=pltpu.CompilerParams(vmem_limit_bytes=16 * 2**20),
        name="unpack_grads",
    )(grads)


def group_sum(value):
    count = lax.axis_size("grp")
    step = 1
    while step < count:
        value = value + lax.ppermute(value, "grp", [(i, i ^ step) for i in range(count)])
        step *= 2
    return value


def per_device(queries, attn_keys, attn_values, byte_grads, seg_starts, up_gain):
    packed = pack(queries, attn_keys, attn_values, byte_grads, seg_starts, 4)
    received = lax.all_to_all(packed, "seq", split_axis=0, concat_axis=0, tiled=True)
    gain = lax.dynamic_slice_in_dim(up_gain.reshape(-1, HD), lax.axis_index("seq"), 1)
    grads, gain_grad = attention(received, gain, 256)
    returned = lax.all_to_all(grads, "seq", split_axis=0, concat_axis=0, tiled=True)
    dq, dk, dv = unpack(returned)
    return dq, dk, dv, group_sum(gain_grad).reshape(HD)


def solution(mesh):
    rows = P("grp", "seq", None)
    return jax.shard_map(
        per_device,
        mesh=mesh,
        in_specs=(rows, rows, rows, rows, rows, P()),
        out_specs=(rows, rows, rows, P("seq")),
        check_vma=False,
    )
```

```python
import functools
import math

import jax
import jax.numpy as jnp
from jax import lax
from jax.experimental import pallas as pl
from jax.experimental.pallas import tpu as pltpu
from jax.sharding import PartitionSpec as P

HD = 128
EXTRA = 8


def start_columns(starts, byte_count):
    count = starts.shape[1]
    row = lax.broadcasted_iota(jnp.int32, (count, count), 0)
    col = lax.broadcasted_iota(jnp.int32, (count, count), 1)
    spread = jnp.broadcast_to(starts, (count, count))
    begin = jnp.sum(jnp.where(row == col, spread, 0), axis=1, keepdims=True)
    end = jnp.sum(jnp.where(row + 1 == col, spread, 0), axis=1, keepdims=True)
    last_row = lax.broadcasted_iota(jnp.int32, (count, 1), 0) == count - 1
    return begin, jnp.where(last_row, byte_count, end)


def pack_kernel(query_ref, key_ref, value_ref, bytes_ref, starts_ref, packed_ref):
    heads = packed_ref.shape[0]
    slots = query_ref.shape[1]
    byte_count = bytes_ref.shape[1]
    starts = starts_ref[0].astype(jnp.float32)
    begin, end = start_columns(starts, float(byte_count))
    position = lax.broadcasted_iota(jnp.int32, (slots, byte_count), 1).astype(jnp.float32)
    own = (begin <= position) & (position < end)
    filled = jnp.sum(jnp.where(starts < byte_count, 1.0, 0.0), axis=1, keepdims=True)
    first = jnp.min(starts, axis=1, keepdims=True)
    last = jnp.max(jnp.where(starts < byte_count, starts, -1.0), axis=1, keepdims=True)
    row = lax.broadcasted_iota(jnp.int32, (EXTRA, byte_count), 0)
    place = lax.broadcasted_iota(jnp.int32, (EXTRA, byte_count), 1).astype(jnp.float32)
    leading = (row < 2) & (place < first)
    tail = (row == 2) & (place >= last)
    member = jnp.concatenate(
        [jnp.where(own, 1.0, 0.0), jnp.where(leading | tail, 1.0, 0.0)], axis=0
    ).astype(jnp.bfloat16)
    sums = jnp.dot(member, bytes_ref[0], preferred_element_type=jnp.float32)
    extra = sums[slots:]
    low = extra - extra.astype(jnp.bfloat16).astype(jnp.float32)
    kind = lax.broadcasted_iota(jnp.int32, extra.shape, 0)
    extra = jnp.where(kind == 0, extra, jnp.where(kind == 3, filled, low)).astype(jnp.bfloat16)
    pooled = sums[:slots].astype(jnp.bfloat16)
    for head in range(heads):
        cols = slice(head * HD, (head + 1) * HD)
        packed_ref[head, 0:slots, :] = query_ref[0, :, cols]
        packed_ref[head, slots : 2 * slots, :] = key_ref[0, :, cols]
        packed_ref[head, 2 * slots : 3 * slots, :] = value_ref[0, :, cols]
        packed_ref[head, 3 * slots : 4 * slots, :] = pooled[:, cols]
        packed_ref[head, 4 * slots :, :] = extra[:, cols]


def pack(queries, attn_keys, attn_values, byte_grads, seg_starts, steps):
    slots, width = queries.shape[1:]
    byte_count = byte_grads.shape[1]
    cap = seg_starts.shape[2]
    cols = width // steps
    heads = width // HD
    rows = 4 * slots + EXTRA
    slot_spec = pl.BlockSpec((1, slots, cols), lambda i: (0, 0, i))
    return pl.pallas_call(
        pack_kernel,
        grid=(steps,),
        in_specs=[
            slot_spec,
            slot_spec,
            slot_spec,
            pl.BlockSpec((1, byte_count, cols), lambda i: (0, 0, i)),
            pl.BlockSpec((1, 1, cap), lambda i: (0, 0, 0)),
        ],
        out_specs=pl.BlockSpec((heads // steps, rows, HD), lambda i: (i, 0, 0)),
        out_shape=jax.ShapeDtypeStruct((heads, rows, HD), jnp.bfloat16),
        compiler_params=pltpu.CompilerParams(vmem_limit_bytes=60 * 2**20),
        name="pool_and_pack",
    )(queries, attn_keys, attn_values, byte_grads, seg_starts)


def attention_kernel(
    block,
    packed_ref,
    gain_ref,
    grads_ref,
    gain_grad_ref,
    upstream_ref,
    pooled_ref,
    bias_ref,
    dk_ref,
    dv_ref,
    staged_ref,
    sems,
):
    shards, rows, width = packed_ref.shape
    slots = (rows - EXTRA) // 4
    total = shards * slots
    scaling = 1.0 / math.sqrt(width)

    extra = packed_ref[:, 4 * slots :, :].astype(jnp.float32)
    carried = extra[:, 0:1, :] + extra[:, 1:2, :]
    incoming = jnp.concatenate([carried[1:], jnp.zeros_like(carried[:1])], axis=0)
    incoming = incoming + extra[:, 2:3, :]
    filled = extra[:, 3:4, :]
    slot = lax.broadcasted_iota(jnp.int32, (shards, slots, width), 1).astype(jnp.float32)
    pooled = packed_ref[:, 3 * slots : 4 * slots, :].astype(jnp.float32)
    pooled = pooled + jnp.where(slot == filled - 1.0, incoming, 0.0)
    pooled = pooled.reshape(total, width).astype(jnp.bfloat16)
    pooled_ref[...] = pooled
    upstream_ref[...] = (gain_ref[...] * pooled.astype(jnp.float32)).astype(jnp.bfloat16)
    bias_ref[...] = jnp.where(slot < filled, 0.0, -1e30).reshape(total, width)

    query = packed_ref[:, 0:slots, :].reshape(total, width)
    key = packed_ref[:, slots : 2 * slots, :].reshape(total, width)
    value = packed_ref[:, 2 * slots : 3 * slots, :].reshape(total, width)
    key_t = key.T
    value_t = value.T
    gain_grad = jnp.zeros((1, width), jnp.float32)
    contract_last = (((1,), (1,)), ((), ()))
    blocks = total // block
    copies = []
    for index in reversed(range(blocks)):
        first = index * block
        prefix = first + block
        query_block = query[first:prefix]
        upstream_block = upstream_ref[first:prefix]
        scores = lax.dot_general(
            key[:prefix], query_block, contract_last, preferred_element_type=jnp.float32
        )
        bias = jnp.concatenate([bias_ref[:prefix]] * (block // width), axis=1)
        scores = scores + bias
        key_ids = lax.broadcasted_iota(jnp.int32, (block, block), 0)
        query_ids = lax.broadcasted_iota(jnp.int32, (block, block), 1)
        diagonal = jnp.where(key_ids <= query_ids, scores[first:], -1e30)
        scores = jnp.concatenate([scores[:first], diagonal], axis=0) if first else diagonal
        row_max = jnp.max(scores, axis=0, keepdims=True)
        weights = jnp.exp((scores - row_max) * scaling)
        probs = weights * (1.0 / jnp.sum(weights, axis=0, keepdims=True))
        probs_low = probs.astype(jnp.bfloat16)
        out_t = jnp.dot(value_t[:, :prefix], probs_low, preferred_element_type=jnp.float32)
        out_t = out_t.astype(jnp.bfloat16).astype(jnp.float32)
        upstream_t = upstream_block.astype(jnp.float32).T
        row_delta = jnp.sum(upstream_t * out_t, axis=0, keepdims=True)
        gain_grad += jnp.sum(
            out_t.T * pooled_ref[first:prefix].astype(jnp.float32), axis=0, keepdims=True
        )
        grad_probs = lax.dot_general(
            value[:prefix], upstream_block, contract_last, preferred_element_type=jnp.float32
        )
        grad_scores = (probs * (grad_probs - row_delta)).astype(jnp.bfloat16)
        dq_t = jnp.dot(key_t[:, :prefix], grad_scores, preferred_element_type=jnp.float32)
        dk = jnp.dot(grad_scores, query_block, preferred_element_type=jnp.float32)
        dv = jnp.dot(probs_low, upstream_block, preferred_element_type=jnp.float32)
        dk_own, dv_own = dk[first:], dv[first:]
        if index < blocks - 1:
            dk_own = dk_own + dk_ref[first:prefix]
            dv_own = dv_own + dv_ref[first:prefix]
        if first and index < blocks - 1:
            dk_ref[:first] += dk[:first]
            dv_ref[:first] += dv[:first]
        elif first:
            dk_ref[:first] = dk[:first]
            dv_ref[:first] = dv[:first]
        owners = slice(first // slots, prefix // slots)
        shape = (block // slots, slots, width)
        staged_ref[owners, 0:slots, :] = (dq_t.T * scaling).astype(jnp.bfloat16).reshape(shape)
        staged_ref[owners, slots : 2 * slots, :] = (
            (dk_own * scaling).astype(jnp.bfloat16).reshape(shape)
        )
        staged_ref[owners, 2 * slots :, :] = dv_own.astype(jnp.bfloat16).reshape(shape)
        copy = pltpu.make_async_copy(
            staged_ref.at[owners], grads_ref.at[owners], sems.at[index]
        )
        copy.start()
        copies.append(copy)
    gain_grad_ref[...] = gain_grad
    for copy in copies:
        copy.wait()


def attention(packed, gain, block):
    shards, rows, width = packed.shape
    slots = (rows - EXTRA) // 4
    total = shards * slots
    vmem = pl.BlockSpec(memory_space=pltpu.VMEM)
    return pl.pallas_call(
        functools.partial(attention_kernel, block),
        in_specs=[vmem, vmem],
        out_specs=[pl.BlockSpec(memory_space=pl.ANY), vmem],
        out_shape=[
            jax.ShapeDtypeStruct((shards, 3 * slots, width), jnp.bfloat16),
            jax.ShapeDtypeStruct((1, width), jnp.float32),
        ],
        scratch_shapes=[
            pltpu.VMEM((total, width), jnp.bfloat16),
            pltpu.VMEM((total, width), jnp.bfloat16),
            pltpu.VMEM((total, width), jnp.float32),
            pltpu.VMEM((total, width), jnp.float32),
            pltpu.VMEM((total, width), jnp.float32),
            pltpu.VMEM((shards, 3 * slots, width), jnp.bfloat16),
            pltpu.SemaphoreType.DMA((total // block,)),
        ],
        compiler_params=pltpu.CompilerParams(vmem_limit_bytes=40 * 2**20),
        name="attention_grads",
    )(packed, gain)


def unpack_kernel(grads_ref, dq_ref, dk_ref, dv_ref):
    slots = dq_ref.shape[1]
    for head in range(grads_ref.shape[0]):
        cols = slice(head * HD, (head + 1) * HD)
        dq_ref[0, :, cols] = grads_ref[head, 0:slots, :]
        dk_ref[0, :, cols] = grads_ref[head, slots : 2 * slots, :]
        dv_ref[0, :, cols] = grads_ref[head, 2 * slots :, :]


def unpack(grads):
    heads, rows, width = grads.shape
    out = jax.ShapeDtypeStruct((1, rows // 3, heads * width), jnp.bfloat16)
    vmem = pl.BlockSpec(memory_space=pltpu.VMEM)
    return pl.pallas_call(
        unpack_kernel,
        in_specs=[vmem],
        out_specs=[vmem] * 3,
        out_shape=[out] * 3,
        compiler_params=pltpu.CompilerParams(vmem_limit_bytes=16 * 2**20),
        name="unpack_grads",
    )(grads)


def group_half(value, step):
    count = lax.axis_size("grp")
    return lax.ppermute(value, "grp", [(i, i ^ step) for i in range(count)])


def per_device(queries, attn_keys, attn_values, byte_grads, seg_starts, up_gain):
    packed = pack(queries, attn_keys, attn_values, byte_grads, seg_starts, 2)
    received = lax.all_to_all(packed, "seq", split_axis=0, concat_axis=0, tiled=True)
    gain = lax.dynamic_slice_in_dim(up_gain.reshape(-1, HD), lax.axis_index("seq"), 1)
    grads, gain_grad = attention(received, gain, 512)
    returned = lax.all_to_all(grads, "seq", split_axis=0, concat_axis=0, tiled=True)
    step = lax.axis_size("grp") // 2
    while step > 1:
        gain_grad = gain_grad + group_half(gain_grad, step)
        step //= 2
    other = group_half(gain_grad, step)
    dq, dk, dv = unpack(returned)
    gain_grad, dv = lax.optimization_barrier((gain_grad, dv))
    return dq, dk, dv, (gain_grad + other).reshape(HD)


def solution(mesh):
    rows = P("grp", "seq", None)
    return jax.shard_map(
        per_device,
        mesh=mesh,
        in_specs=(rows, rows, rows, rows, rows, P()),
        out_specs=(rows, rows, rows, P("seq")),
        check_vma=False,
    )
```

```python
import functools
import math

import jax
import jax.numpy as jnp
from jax import lax
from jax.experimental import pallas as pl
from jax.experimental.pallas import tpu as pltpu
from jax.sharding import PartitionSpec as P

HD = 128
EXTRA = 8


def start_columns(starts, byte_count):
    count = starts.shape[1]
    row = lax.broadcasted_iota(jnp.int32, (count, count), 0)
    col = lax.broadcasted_iota(jnp.int32, (count, count), 1)
    spread = jnp.broadcast_to(starts, (count, count))
    begin = jnp.sum(jnp.where(row == col, spread, 0), axis=1, keepdims=True)
    end = jnp.sum(jnp.where(row + 1 == col, spread, 0), axis=1, keepdims=True)
    last_row = lax.broadcasted_iota(jnp.int32, (count, 1), 0) == count - 1
    return begin, jnp.where(last_row, byte_count, end)


def pack_kernel(query_ref, key_ref, value_ref, bytes_ref, starts_ref, packed_ref):
    heads = packed_ref.shape[0]
    slots = query_ref.shape[1]
    byte_count = bytes_ref.shape[1]
    starts = starts_ref[0].astype(jnp.float32)
    begin, end = start_columns(starts, float(byte_count))
    position = lax.broadcasted_iota(jnp.int32, (slots, byte_count), 1).astype(jnp.float32)
    own = (begin <= position) & (position < end)
    filled = jnp.sum(jnp.where(starts < byte_count, 1.0, 0.0), axis=1, keepdims=True)
    first = jnp.min(starts, axis=1, keepdims=True)
    last = jnp.max(jnp.where(starts < byte_count, starts, -1.0), axis=1, keepdims=True)
    row = lax.broadcasted_iota(jnp.int32, (EXTRA, byte_count), 0)
    place = lax.broadcasted_iota(jnp.int32, (EXTRA, byte_count), 1).astype(jnp.float32)
    leading = (row < 2) & (place < first)
    tail = (row == 2) & (place >= last)
    member = jnp.concatenate(
        [jnp.where(own, 1.0, 0.0), jnp.where(leading | tail, 1.0, 0.0)], axis=0
    ).astype(jnp.bfloat16)
    sums = jnp.dot(member, bytes_ref[0], preferred_element_type=jnp.float32)
    extra = sums[slots:]
    low = extra - extra.astype(jnp.bfloat16).astype(jnp.float32)
    kind = lax.broadcasted_iota(jnp.int32, extra.shape, 0)
    extra = jnp.where(kind == 0, extra, jnp.where(kind == 3, filled, low)).astype(jnp.bfloat16)
    pooled = sums[:slots].astype(jnp.bfloat16)
    for head in range(heads):
        cols = slice(head * HD, (head + 1) * HD)
        packed_ref[head, 0:slots, :] = query_ref[0, :, cols]
        packed_ref[head, slots : 2 * slots, :] = key_ref[0, :, cols]
        packed_ref[head, 2 * slots : 3 * slots, :] = value_ref[0, :, cols]
        packed_ref[head, 3 * slots : 4 * slots, :] = pooled[:, cols]
        packed_ref[head, 4 * slots :, :] = extra[:, cols]


def pack(queries, attn_keys, attn_values, byte_grads, seg_starts, steps):
    slots, width = queries.shape[1:]
    byte_count = byte_grads.shape[1]
    cap = seg_starts.shape[2]
    cols = width // steps
    heads = width // HD
    rows = 4 * slots + EXTRA
    slot_spec = pl.BlockSpec((1, slots, cols), lambda i: (0, 0, i))
    return pl.pallas_call(
        pack_kernel,
        grid=(steps,),
        in_specs=[
            slot_spec,
            slot_spec,
            slot_spec,
            pl.BlockSpec((1, byte_count, cols), lambda i: (0, 0, i)),
            pl.BlockSpec((1, 1, cap), lambda i: (0, 0, 0)),
        ],
        out_specs=pl.BlockSpec((heads // steps, rows, HD), lambda i: (i, 0, 0)),
        out_shape=jax.ShapeDtypeStruct((heads, rows, HD), jnp.bfloat16),
        compiler_params=pltpu.CompilerParams(vmem_limit_bytes=60 * 2**20),
        name="pool_and_pack",
    )(queries, attn_keys, attn_values, byte_grads, seg_starts)


def dot(left, right):
    return jnp.dot(left, right, preferred_element_type=jnp.float32)


def dot_t(left, right):
    contract_last = (((1,), (1,)), ((), ()))
    return lax.dot_general(left, right, contract_last, preferred_element_type=jnp.float32)


def add_late(combine, wide, late):
    half = late.shape[1]
    return jnp.concatenate([wide[:, :half], combine(wide[:, half:], late)], axis=1)


def attention_kernel(
    block,
    packed_ref,
    gain_ref,
    grads_ref,
    gain_grad_ref,
    upstream_ref,
    pooled_ref,
    bias_ref,
    dk_ref,
    dv_ref,
    staged_ref,
    sems,
):
    shards, rows, width = packed_ref.shape
    slots = (rows - EXTRA) // 4
    total = shards * slots
    scaling = 1.0 / math.sqrt(width)

    extra = packed_ref[:, 4 * slots :, :].astype(jnp.float32)
    carried = extra[:, 0:1, :] + extra[:, 1:2, :]
    incoming = jnp.concatenate([carried[1:], jnp.zeros_like(carried[:1])], axis=0)
    incoming = incoming + extra[:, 2:3, :]
    filled = extra[:, 3:4, :]
    slot = lax.broadcasted_iota(jnp.int32, (shards, slots, width), 1).astype(jnp.float32)
    pooled = packed_ref[:, 3 * slots : 4 * slots, :].astype(jnp.float32)
    pooled = pooled + jnp.where(slot == filled - 1.0, incoming, 0.0)
    pooled = pooled.reshape(total, width).astype(jnp.bfloat16)
    pooled_ref[...] = pooled
    upstream_ref[...] = (gain_ref[...] * pooled.astype(jnp.float32)).astype(jnp.bfloat16)
    bias_ref[...] = jnp.where(slot < filled, 0.0, -1e30).reshape(total, width)

    query = packed_ref[:, 0:slots, :].reshape(total, width)
    key = packed_ref[:, slots : 2 * slots, :].reshape(total, width)
    value = packed_ref[:, 2 * slots : 3 * slots, :].reshape(total, width)
    key_t = key.T
    value_t = value.T
    gain_grad = jnp.zeros((1, width), jnp.float32)
    half = block // 2
    causal = lax.broadcasted_iota(jnp.int32, (half, half), 0) <= lax.broadcasted_iota(
        jnp.int32, (half, half), 1
    )
    blocks = total // block
    copies = []
    for index in reversed(range(blocks)):
        first = index * block
        middle = first + half
        prefix = first + block
        query_block = query[first:prefix]
        upstream_block = upstream_ref[first:prefix]
        wide = dot_t(key[:middle], query_block)
        late = dot_t(key[middle:prefix], query_block[half:])
        wide = wide + jnp.concatenate([bias_ref[:middle]] * (block // width), axis=1)
        late = late + jnp.concatenate([bias_ref[middle:prefix]] * (half // width), axis=1)
        late = jnp.where(causal, late, -1e30)
        square = jnp.where(causal, wide[first:, :half], -1e30)
        square = jnp.concatenate([square, wide[first:, half:]], axis=1)
        wide = jnp.concatenate([wide[:first], square], axis=0) if first else square
        row_max = add_late(
            jnp.maximum, jnp.max(wide, axis=0, keepdims=True), jnp.max(late, axis=0, keepdims=True)
        )
        wide = jnp.exp((wide - row_max) * scaling)
        late = jnp.exp((late - row_max[:, half:]) * scaling)
        inverse = 1.0 / add_late(
            jnp.add, jnp.sum(wide, axis=0, keepdims=True), jnp.sum(late, axis=0, keepdims=True)
        )
        wide_probs = wide * inverse
        late_probs = late * inverse[:, half:]
        wide_low = wide_probs.astype(jnp.bfloat16)
        late_low = late_probs.astype(jnp.bfloat16)
        out_t = add_late(
            jnp.add, dot(value_t[:, :middle], wide_low), dot(value_t[:, middle:prefix], late_low)
        )
        out_t = out_t.astype(jnp.bfloat16).astype(jnp.float32)
        upstream_t = upstream_block.astype(jnp.float32).T
        row_delta = jnp.sum(upstream_t * out_t, axis=0, keepdims=True)
        gain_grad += jnp.sum(
            out_t.T * pooled_ref[first:prefix].astype(jnp.float32), axis=0, keepdims=True
        )
        wide_grad = dot_t(value[:middle], upstream_block) - row_delta
        late_grad = dot_t(value[middle:prefix], upstream_block[half:]) - row_delta[:, half:]
        wide_grad = (wide_probs * wide_grad).astype(jnp.bfloat16)
        late_grad = (late_probs * late_grad).astype(jnp.bfloat16)
        dq_t = add_late(
            jnp.add, dot(key_t[:, :middle], wide_grad), dot(key_t[:, middle:prefix], late_grad)
        )
        dk = dot(wide_grad, query_block)
        dv = dot(wide_low, upstream_block)
        dk_own = jnp.concatenate([dk[first:], dot(late_grad, query_block[half:])], axis=0)
        dv_own = jnp.concatenate([dv[first:], dot(late_low, upstream_block[half:])], axis=0)
        if index < blocks - 1:
            dk_own = dk_own + dk_ref[first:prefix]
            dv_own = dv_own + dv_ref[first:prefix]
        if first and index < blocks - 1:
            dk_ref[:first] += dk[:first]
            dv_ref[:first] += dv[:first]
        elif first:
            dk_ref[:first] = dk[:first]
            dv_ref[:first] = dv[:first]
        owners = slice(first // slots, prefix // slots)
        shape = (block // slots, slots, width)
        staged_ref[owners, 0:slots, :] = (dq_t.T * scaling).astype(jnp.bfloat16).reshape(shape)
        staged_ref[owners, slots : 2 * slots, :] = (
            (dk_own * scaling).astype(jnp.bfloat16).reshape(shape)
        )
        staged_ref[owners, 2 * slots :, :] = dv_own.astype(jnp.bfloat16).reshape(shape)
        copy = pltpu.make_async_copy(
            staged_ref.at[owners], grads_ref.at[owners], sems.at[index]
        )
        copy.start()
        copies.append(copy)
    gain_grad_ref[...] = gain_grad
    for copy in copies:
        copy.wait()


def attention(packed, gain, block):
    shards, rows, width = packed.shape
    slots = (rows - EXTRA) // 4
    total = shards * slots
    vmem = pl.BlockSpec(memory_space=pltpu.VMEM)
    return pl.pallas_call(
        functools.partial(attention_kernel, block),
        in_specs=[vmem, vmem],
        out_specs=[pl.BlockSpec(memory_space=pl.ANY), vmem],
        out_shape=[
            jax.ShapeDtypeStruct((shards, 3 * slots, width), jnp.bfloat16),
            jax.ShapeDtypeStruct((1, width), jnp.float32),
        ],
        scratch_shapes=[
            pltpu.VMEM((total, width), jnp.bfloat16),
            pltpu.VMEM((total, width), jnp.bfloat16),
            pltpu.VMEM((total, width), jnp.float32),
            pltpu.VMEM((total, width), jnp.float32),
            pltpu.VMEM((total, width), jnp.float32),
            pltpu.VMEM((shards, 3 * slots, width), jnp.bfloat16),
            pltpu.SemaphoreType.DMA((total // block,)),
        ],
        compiler_params=pltpu.CompilerParams(vmem_limit_bytes=40 * 2**20),
        name="attention_grads",
    )(packed, gain)


def unpack_kernel(grads_ref, dq_ref, dk_ref, dv_ref):
    slots = dq_ref.shape[1]
    for head in range(grads_ref.shape[0]):
        cols = slice(head * HD, (head + 1) * HD)
        dq_ref[0, :, cols] = grads_ref[head, 0:slots, :]
        dk_ref[0, :, cols] = grads_ref[head, slots : 2 * slots, :]
        dv_ref[0, :, cols] = grads_ref[head, 2 * slots :, :]


def unpack(grads):
    heads, rows, width = grads.shape
    out = jax.ShapeDtypeStruct((1, rows // 3, heads * width), jnp.bfloat16)
    vmem = pl.BlockSpec(memory_space=pltpu.VMEM)
    return pl.pallas_call(
        unpack_kernel,
        in_specs=[vmem],
        out_specs=[vmem] * 3,
        out_shape=[out] * 3,
        compiler_params=pltpu.CompilerParams(vmem_limit_bytes=16 * 2**20),
        name="unpack_grads",
    )(grads)


def group_half(value, step):
    count = lax.axis_size("grp")
    return lax.ppermute(value, "grp", [(i, i ^ step) for i in range(count)])


def per_device(queries, attn_keys, attn_values, byte_grads, seg_starts, up_gain):
    packed = pack(queries, attn_keys, attn_values, byte_grads, seg_starts, 2)
    received = lax.all_to_all(packed, "seq", split_axis=0, concat_axis=0, tiled=True)
    gain = lax.dynamic_slice_in_dim(up_gain.reshape(-1, HD), lax.axis_index("seq"), 1)
    grads, gain_grad = attention(received, gain, 512)
    returned = lax.all_to_all(grads, "seq", split_axis=0, concat_axis=0, tiled=True)
    step = lax.axis_size("grp") // 2
    while step > 1:
        gain_grad = gain_grad + group_half(gain_grad, step)
        step //= 2
    other = group_half(gain_grad, step)
    dq, dk, dv = unpack(returned)
    gain_grad, dv = lax.optimization_barrier((gain_grad, dv))
    return dq, dk, dv, (gain_grad + other).reshape(HD)


def solution(mesh):
    rows = P("grp", "seq", None)
    return jax.shard_map(
        per_device,
        mesh=mesh,
        in_specs=(rows, rows, rows, rows, rows, P()),
        out_specs=(rows, rows, rows, P("seq")),
        check_vma=False,
    )
```

```python
import functools
import math

import jax
import jax.numpy as jnp
from jax import lax
from jax.experimental import pallas as pl
from jax.experimental.pallas import tpu as pltpu
from jax.sharding import PartitionSpec as P

HD = 128
EXTRA = 8


def start_columns(starts, byte_count):
    count = starts.shape[1]
    row = lax.broadcasted_iota(jnp.int32, (count, count), 0)
    col = lax.broadcasted_iota(jnp.int32, (count, count), 1)
    spread = jnp.broadcast_to(starts, (count, count))
    begin = jnp.sum(jnp.where(row == col, spread, 0), axis=1, keepdims=True)
    end = jnp.sum(jnp.where(row + 1 == col, spread, 0), axis=1, keepdims=True)
    last_row = lax.broadcasted_iota(jnp.int32, (count, 1), 0) == count - 1
    return begin, jnp.where(last_row, byte_count, end)


def pack_kernel(query_ref, key_ref, value_ref, bytes_ref, starts_ref, packed_ref):
    heads = packed_ref.shape[0]
    slots = query_ref.shape[1]
    byte_count = bytes_ref.shape[1]
    starts = starts_ref[0].astype(jnp.float32)
    begin, end = start_columns(starts, float(byte_count))
    position = lax.broadcasted_iota(jnp.int32, (slots, byte_count), 1).astype(jnp.float32)
    own = (begin <= position) & (position < end)
    filled = jnp.sum(jnp.where(starts < byte_count, 1.0, 0.0), axis=1, keepdims=True)
    first = jnp.min(starts, axis=1, keepdims=True)
    last = jnp.max(jnp.where(starts < byte_count, starts, -1.0), axis=1, keepdims=True)
    row = lax.broadcasted_iota(jnp.int32, (EXTRA, byte_count), 0)
    place = lax.broadcasted_iota(jnp.int32, (EXTRA, byte_count), 1).astype(jnp.float32)
    leading = (row < 2) & (place < first)
    tail = (row == 2) & (place >= last)
    member = jnp.concatenate(
        [jnp.where(own, 1.0, 0.0), jnp.where(leading | tail, 1.0, 0.0)], axis=0
    ).astype(jnp.bfloat16)
    sums = jnp.dot(member, bytes_ref[0], preferred_element_type=jnp.float32)
    extra = sums[slots:]
    low = extra - extra.astype(jnp.bfloat16).astype(jnp.float32)
    kind = lax.broadcasted_iota(jnp.int32, extra.shape, 0)
    extra = jnp.where(kind == 0, extra, jnp.where(kind == 3, filled, low)).astype(jnp.bfloat16)
    pooled = sums[:slots].astype(jnp.bfloat16)
    for head in range(heads):
        cols = slice(head * HD, (head + 1) * HD)
        packed_ref[head, 0:slots, :] = query_ref[0, :, cols]
        packed_ref[head, slots : 2 * slots, :] = key_ref[0, :, cols]
        packed_ref[head, 2 * slots : 3 * slots, :] = value_ref[0, :, cols]
        packed_ref[head, 3 * slots : 4 * slots, :] = pooled[:, cols]
        packed_ref[head, 4 * slots :, :] = extra[:, cols]


def pack(queries, attn_keys, attn_values, byte_grads, seg_starts, steps):
    slots, width = queries.shape[1:]
    byte_count = byte_grads.shape[1]
    cap = seg_starts.shape[2]
    cols = width // steps
    heads = width // HD
    rows = 4 * slots + EXTRA
    slot_spec = pl.BlockSpec((1, slots, cols), lambda i: (0, 0, i))
    return pl.pallas_call(
        pack_kernel,
        grid=(steps,),
        in_specs=[
            slot_spec,
            slot_spec,
            slot_spec,
            pl.BlockSpec((1, byte_count, cols), lambda i: (0, 0, i)),
            pl.BlockSpec((1, 1, cap), lambda i: (0, 0, 0)),
        ],
        out_specs=pl.BlockSpec((heads // steps, rows, HD), lambda i: (i, 0, 0)),
        out_shape=jax.ShapeDtypeStruct((heads, rows, HD), jnp.bfloat16),
        compiler_params=pltpu.CompilerParams(vmem_limit_bytes=60 * 2**20),
        name="pool_and_pack",
    )(queries, attn_keys, attn_values, byte_grads, seg_starts)


def dot(left, right):
    return jnp.dot(left, right, preferred_element_type=jnp.float32)


def dot_t(left, right):
    contract_last = (((1,), (1,)), ((), ()))
    return lax.dot_general(left, right, contract_last, preferred_element_type=jnp.float32)


def add_late(combine, wide, late):
    half = late.shape[1]
    return jnp.concatenate([wide[:, :half], combine(wide[:, half:], late)], axis=1)


def attention_kernel(
    block,
    packed_ref,
    gain_ref,
    grads_ref,
    gain_grad_ref,
    upstream_ref,
    pooled_ref,
    bias_ref,
    dk_ref,
    dv_ref,
    staged_ref,
    sems,
):
    shards, rows, width = packed_ref.shape
    slots = (rows - EXTRA) // 4
    total = shards * slots
    scaling = 1.0 / math.sqrt(width)

    extra = packed_ref[:, 4 * slots :, :].astype(jnp.float32)
    carried = extra[:, 0:1, :] + extra[:, 1:2, :]
    incoming = jnp.concatenate([carried[1:], jnp.zeros_like(carried[:1])], axis=0)
    incoming = incoming + extra[:, 2:3, :]
    filled = extra[:, 3:4, :]
    slot = lax.broadcasted_iota(jnp.int32, (shards, slots, width), 1).astype(jnp.float32)
    pooled = packed_ref[:, 3 * slots : 4 * slots, :].astype(jnp.float32)
    pooled = pooled + jnp.where(slot == filled - 1.0, incoming, 0.0)
    pooled = pooled.reshape(total, width).astype(jnp.bfloat16)
    pooled_ref[...] = pooled
    upstream_ref[...] = (gain_ref[...] * pooled.astype(jnp.float32)).astype(jnp.bfloat16)
    bias_ref[...] = jnp.where(slot < filled, 0.0, -1e30).reshape(total, width)

    query = packed_ref[:, 0:slots, :].reshape(total, width)
    key = packed_ref[:, slots : 2 * slots, :].reshape(total, width)
    value = packed_ref[:, 2 * slots : 3 * slots, :].reshape(total, width)
    key_t = key.T
    value_t = value.T
    gain_grad = jnp.zeros((1, width), jnp.float32)
    half = block // 2
    causal = lax.broadcasted_iota(jnp.int32, (half, half), 0) <= lax.broadcasted_iota(
        jnp.int32, (half, half), 1
    )
    blocks = total // block
    copies = []
    for index in reversed(range(blocks)):
        first = index * block
        middle = first + half
        prefix = first + block
        query_block = query[first:prefix]
        upstream_block = upstream_ref[first:prefix]
        wide = dot_t(key[:middle], query_block)
        late = dot_t(key[middle:prefix], query_block[half:])
        wide = wide + jnp.concatenate([bias_ref[:middle]] * (block // width), axis=1)
        late = late + jnp.concatenate([bias_ref[middle:prefix]] * (half // width), axis=1)
        late = jnp.where(causal, late, -1e30)
        square = jnp.where(causal, wide[first:, :half], -1e30)
        square = jnp.concatenate([square, wide[first:, half:]], axis=1)
        wide = jnp.concatenate([wide[:first], square], axis=0) if first else square
        row_max = add_late(
            jnp.maximum, jnp.max(wide, axis=0, keepdims=True), jnp.max(late, axis=0, keepdims=True)
        )
        wide = jnp.exp((wide - row_max) * scaling)
        late = jnp.exp((late - row_max[:, half:]) * scaling)
        inverse = 1.0 / add_late(
            jnp.add, jnp.sum(wide, axis=0, keepdims=True), jnp.sum(late, axis=0, keepdims=True)
        )
        wide_probs = wide * inverse
        late_probs = late * inverse[:, half:]
        wide_low = wide_probs.astype(jnp.bfloat16)
        late_low = late_probs.astype(jnp.bfloat16)
        owners = slice(first // slots, prefix // slots)
        shape = (block // slots, slots, width)

        def send(kind, array):
            rows = slice(kind * slots, (kind + 1) * slots)
            staged_ref[owners, rows, :] = array.astype(jnp.bfloat16).reshape(shape)
            copy = pltpu.make_async_copy(
                staged_ref.at[owners, rows], grads_ref.at[owners, rows], sems.at[index, kind]
            )
            copy.start()
            copies.append(copy)

        dv = dot(wide_low, upstream_block)
        dv_own = jnp.concatenate([dv[first:], dot(late_low, upstream_block[half:])], axis=0)
        if index < blocks - 1:
            dv_own = dv_own + dv_ref[first:prefix]
        if first and index < blocks - 1:
            dv_ref[:first] += dv[:first]
        elif first:
            dv_ref[:first] = dv[:first]
        send(2, dv_own)
        out_t = add_late(
            jnp.add, dot(value_t[:, :middle], wide_low), dot(value_t[:, middle:prefix], late_low)
        )
        out_t = out_t.astype(jnp.bfloat16).astype(jnp.float32)
        upstream_t = upstream_block.astype(jnp.float32).T
        row_delta = jnp.sum(upstream_t * out_t, axis=0, keepdims=True)
        gain_grad += jnp.sum(
            out_t.T * pooled_ref[first:prefix].astype(jnp.float32), axis=0, keepdims=True
        )
        wide_grad = dot_t(value[:middle], upstream_block) - row_delta
        late_grad = dot_t(value[middle:prefix], upstream_block[half:]) - row_delta[:, half:]
        wide_grad = (wide_probs * wide_grad).astype(jnp.bfloat16)
        late_grad = (late_probs * late_grad).astype(jnp.bfloat16)
        dq_t = add_late(
            jnp.add, dot(key_t[:, :middle], wide_grad), dot(key_t[:, middle:prefix], late_grad)
        )
        send(0, dq_t.T * scaling)
        dk = dot(wide_grad, query_block)
        dk_own = jnp.concatenate([dk[first:], dot(late_grad, query_block[half:])], axis=0)
        if index < blocks - 1:
            dk_own = dk_own + dk_ref[first:prefix]
        if first and index < blocks - 1:
            dk_ref[:first] += dk[:first]
        elif first:
            dk_ref[:first] = dk[:first]
        send(1, dk_own * scaling)
    gain_grad_ref[...] = gain_grad
    for copy in copies:
        copy.wait()


def attention(packed, gain, block):
    shards, rows, width = packed.shape
    slots = (rows - EXTRA) // 4
    total = shards * slots
    vmem = pl.BlockSpec(memory_space=pltpu.VMEM)
    return pl.pallas_call(
        functools.partial(attention_kernel, block),
        in_specs=[vmem, vmem],
        out_specs=[pl.BlockSpec(memory_space=pl.ANY), vmem],
        out_shape=[
            jax.ShapeDtypeStruct((shards, 3 * slots, width), jnp.bfloat16),
            jax.ShapeDtypeStruct((1, width), jnp.float32),
        ],
        scratch_shapes=[
            pltpu.VMEM((total, width), jnp.bfloat16),
            pltpu.VMEM((total, width), jnp.bfloat16),
            pltpu.VMEM((total, width), jnp.float32),
            pltpu.VMEM((total, width), jnp.float32),
            pltpu.VMEM((total, width), jnp.float32),
            pltpu.VMEM((shards, 3 * slots, width), jnp.bfloat16),
            pltpu.SemaphoreType.DMA((total // block, 3)),
        ],
        compiler_params=pltpu.CompilerParams(vmem_limit_bytes=40 * 2**20),
        name="attention_grads",
    )(packed, gain)


def unpack_kernel(
    grads_ref, here_ref, other_ref, dq_ref, dk_ref, dv_ref, gain_ref, staged_ref, sum_ref, sems
):
    slots = dq_ref.shape[1]
    sum_ref[...] = here_ref[...] + other_ref[...]
    copies = [pltpu.make_async_copy(sum_ref, gain_ref, sems.at[3])]
    copies[0].start()
    for kind, out_ref in enumerate((dq_ref, dk_ref, dv_ref)):
        for head in range(grads_ref.shape[0]):
            cols = slice(head * HD, (head + 1) * HD)
            rows = slice(kind * slots, (kind + 1) * slots)
            staged_ref[kind, 0, :, cols] = grads_ref[head, rows, :]
        copy = pltpu.make_async_copy(staged_ref.at[kind], out_ref, sems.at[kind])
        copy.start()
        copies.append(copy)
    for copy in copies:
        copy.wait()


def unpack(grads, here, other):
    heads, rows, width = grads.shape
    shape = (1, rows // 3, heads * width)
    vmem = pl.BlockSpec(memory_space=pltpu.VMEM)
    return pl.pallas_call(
        unpack_kernel,
        in_specs=[vmem] * 3,
        out_specs=[pl.BlockSpec(memory_space=pl.ANY)] * 4,
        out_shape=[jax.ShapeDtypeStruct(shape, jnp.bfloat16)] * 3
        + [jax.ShapeDtypeStruct((1, width), jnp.float32)],
        scratch_shapes=[
            pltpu.VMEM((3,) + shape, jnp.bfloat16),
            pltpu.VMEM((1, width), jnp.float32),
            pltpu.SemaphoreType.DMA((4,)),
        ],
        compiler_params=pltpu.CompilerParams(vmem_limit_bytes=16 * 2**20),
        name="unpack_grads",
    )(grads, here, other)


RING_STEPS = (1, 7, 2)


def group_half(value, mask):
    count = lax.axis_size("grp")
    return lax.ppermute(value, "grp", [(i, i ^ mask) for i in range(count)])


def per_device(queries, attn_keys, attn_values, byte_grads, seg_starts, up_gain):
    packed = pack(queries, attn_keys, attn_values, byte_grads, seg_starts, 2)
    received = lax.all_to_all(packed, "seq", split_axis=0, concat_axis=0, tiled=True)
    gain = lax.dynamic_slice_in_dim(up_gain.reshape(-1, HD), lax.axis_index("seq"), 1)
    grads, gain_grad = attention(received, gain, 512)
    returned = lax.all_to_all(grads, "seq", split_axis=0, concat_axis=0, tiled=True)
    for mask in RING_STEPS[:-1]:
        gain_grad = gain_grad + group_half(gain_grad, mask)
    other = group_half(gain_grad, RING_STEPS[-1])
    dq, dk, dv, gain_grad = unpack(returned, gain_grad, other)
    return dq, dk, dv, gain_grad.reshape(HD)


def solution(mesh):
    rows = P("grp", "seq", None)
    return jax.shard_map(
        per_device,
        mesh=mesh,
        in_specs=(rows, rows, rows, rows, rows, P()),
        out_specs=(rows, rows, rows, P("seq")),
        check_vma=False,
    )
```

```python
import functools
import math

import jax
import jax.numpy as jnp
from jax import lax
from jax.experimental import pallas as pl
from jax.experimental.pallas import tpu as pltpu
from jax.sharding import PartitionSpec as P

HD = 128
EXTRA = 8


def start_columns(starts, byte_count):
    count = starts.shape[1]
    row = lax.broadcasted_iota(jnp.int32, (count, count), 0)
    col = lax.broadcasted_iota(jnp.int32, (count, count), 1)
    spread = jnp.broadcast_to(starts, (count, count))
    begin = jnp.sum(jnp.where(row == col, spread, 0), axis=1, keepdims=True)
    end = jnp.sum(jnp.where(row + 1 == col, spread, 0), axis=1, keepdims=True)
    last_row = lax.broadcasted_iota(jnp.int32, (count, 1), 0) == count - 1
    return begin, jnp.where(last_row, byte_count, end)


def pack_kernel(query_ref, key_ref, value_ref, bytes_ref, starts_ref, packed_ref):
    heads = packed_ref.shape[0]
    slots = query_ref.shape[1]
    byte_count = bytes_ref.shape[1]
    starts = starts_ref[0].astype(jnp.float32)
    begin, end = start_columns(starts, float(byte_count))
    position = lax.broadcasted_iota(jnp.int32, (slots, byte_count), 1).astype(jnp.float32)
    own = (begin <= position) & (position < end)
    filled = jnp.sum(jnp.where(starts < byte_count, 1.0, 0.0), axis=1, keepdims=True)
    first = jnp.min(starts, axis=1, keepdims=True)
    last = jnp.max(jnp.where(starts < byte_count, starts, -1.0), axis=1, keepdims=True)
    row = lax.broadcasted_iota(jnp.int32, (EXTRA, byte_count), 0)
    place = lax.broadcasted_iota(jnp.int32, (EXTRA, byte_count), 1).astype(jnp.float32)
    leading = (row < 2) & (place < first)
    tail = (row == 2) & (place >= last)
    member = jnp.concatenate(
        [jnp.where(own, 1.0, 0.0), jnp.where(leading | tail, 1.0, 0.0)], axis=0
    ).astype(jnp.bfloat16)
    sums = jnp.dot(member, bytes_ref[0], preferred_element_type=jnp.float32)
    extra = sums[slots:]
    low = extra - extra.astype(jnp.bfloat16).astype(jnp.float32)
    kind = lax.broadcasted_iota(jnp.int32, extra.shape, 0)
    extra = jnp.where(kind == 0, extra, jnp.where(kind == 3, filled, low)).astype(jnp.bfloat16)
    pooled = sums[:slots].astype(jnp.bfloat16)
    for head in range(heads):
        cols = slice(head * HD, (head + 1) * HD)
        packed_ref[head, 0:slots, :] = query_ref[0, :, cols]
        packed_ref[head, slots : 2 * slots, :] = key_ref[0, :, cols]
        packed_ref[head, 2 * slots : 3 * slots, :] = value_ref[0, :, cols]
        packed_ref[head, 3 * slots : 4 * slots, :] = pooled[:, cols]
        packed_ref[head, 4 * slots :, :] = extra[:, cols]


def pack(queries, attn_keys, attn_values, byte_grads, seg_starts, steps):
    slots, width = queries.shape[1:]
    byte_count = byte_grads.shape[1]
    cap = seg_starts.shape[2]
    cols = width // steps
    heads = width // HD
    rows = 4 * slots + EXTRA
    slot_spec = pl.BlockSpec((1, slots, cols), lambda i: (0, 0, i))
    return pl.pallas_call(
        pack_kernel,
        grid=(steps,),
        in_specs=[
            slot_spec,
            slot_spec,
            slot_spec,
            pl.BlockSpec((1, byte_count, cols), lambda i: (0, 0, i)),
            pl.BlockSpec((1, 1, cap), lambda i: (0, 0, 0)),
        ],
        out_specs=pl.BlockSpec((heads // steps, rows, HD), lambda i: (i, 0, 0)),
        out_shape=jax.ShapeDtypeStruct((heads, rows, HD), jnp.bfloat16),
        compiler_params=pltpu.CompilerParams(vmem_limit_bytes=60 * 2**20),
        name="pool_and_pack",
    )(queries, attn_keys, attn_values, byte_grads, seg_starts)


def dot(left, right):
    return jnp.dot(left, right, preferred_element_type=jnp.float32)


def dot_t(left, right):
    contract_last = (((1,), (1,)), ((), ()))
    return lax.dot_general(left, right, contract_last, preferred_element_type=jnp.float32)


def joined(combine, parts):
    whole = parts[0]
    for part in parts[1:]:
        first = whole.shape[1] - part.shape[1]
        whole = jnp.concatenate([whole[:, :first], combine(whole[:, first:], part)], axis=1)
    return whole


def attention_kernel(
    band,
    packed_ref,
    gain_ref,
    grads_ref,
    gain_grad_ref,
    upstream_ref,
    pooled_ref,
    bias_ref,
    staged_ref,
    sems,
):
    shards, rows, width = packed_ref.shape
    slots = (rows - EXTRA) // 4
    total = shards * slots
    scaling = 1.0 / math.sqrt(width)

    extra = packed_ref[:, 4 * slots :, :].astype(jnp.float32)
    carried = extra[:, 0:1, :] + extra[:, 1:2, :]
    incoming = jnp.concatenate([carried[1:], jnp.zeros_like(carried[:1])], axis=0)
    incoming = incoming + extra[:, 2:3, :]
    filled = extra[:, 3:4, :]
    slot = lax.broadcasted_iota(jnp.int32, (shards, slots, width), 1).astype(jnp.float32)
    pooled = packed_ref[:, 3 * slots : 4 * slots, :].astype(jnp.float32)
    pooled = pooled + jnp.where(slot == filled - 1.0, incoming, 0.0)
    pooled = pooled.reshape(total, width).astype(jnp.bfloat16)
    pooled_ref[...] = pooled
    upstream_ref[...] = (gain_ref[...] * pooled.astype(jnp.float32)).astype(jnp.bfloat16)
    bias_ref[...] = jnp.where(slot < filled, 0.0, -1e30).reshape(total, width)

    query = packed_ref[:, 0:slots, :].reshape(total, width)
    key = packed_ref[:, slots : 2 * slots, :].reshape(total, width)
    value = packed_ref[:, 2 * slots : 3 * slots, :].reshape(total, width)
    key_t = key.T
    value_t = value.T
    causal = lax.broadcasted_iota(jnp.int32, (band, band), 0) <= lax.broadcasted_iota(
        jnp.int32, (band, band), 1
    )
    upstream = upstream_ref[...]
    starts = range(0, total, band)
    copies = []

    def send(kind, first, array):
        owners = slice(first // slots, (first + band) // slots)
        rows = slice(kind * slots, (kind + 1) * slots)
        staged_ref[owners, rows, :] = array.astype(jnp.bfloat16).reshape(-1, slots, width)
        copy = pltpu.make_async_copy(
            staged_ref.at[owners, rows], grads_ref.at[owners, rows], sems.at[first // band, kind]
        )
        copy.start()
        copies.append(copy)

    scores = []
    for first in starts:
        part = dot_t(key[first : first + band], query[first:])
        bias = bias_ref[first : first + band]
        part = part + jnp.concatenate([bias] * ((total - first) // width), axis=1)
        square = jnp.where(causal, part[:, :band], -1e30)
        if first + band < total:
            square = jnp.concatenate([square, part[:, band:]], axis=1)
        scores.append(square)
    grad_probs = [dot_t(value[i : i + band], upstream[i:]) for i in starts]
    row_max = joined(jnp.maximum, [jnp.max(part, axis=0, keepdims=True) for part in scores])
    weights = [
        jnp.exp((part - row_max[:, first:]) * scaling) for first, part in zip(starts, scores)
    ]
    inverse = 1.0 / joined(jnp.add, [jnp.sum(part, axis=0, keepdims=True) for part in weights])
    probs = [part * inverse[:, first:] for first, part in zip(starts, weights)]
    probs_low = [part.astype(jnp.bfloat16) for part in probs]
    out_t = joined(
        jnp.add,
        [dot(value_t[:, i : i + band], part) for i, part in zip(starts, probs_low)],
    )
    for first, part in zip(starts, probs_low):
        send(2, first, dot(part, upstream[first:]))
    out_t = out_t.astype(jnp.bfloat16).astype(jnp.float32)
    row_delta = jnp.sum(upstream.astype(jnp.float32).T * out_t, axis=0, keepdims=True)
    gain_grad_ref[...] = jnp.sum(
        out_t.T * pooled_ref[...].astype(jnp.float32), axis=0, keepdims=True
    )
    grads = []
    for first, part, grad in zip(starts, probs, grad_probs):
        grads.append((part * (grad - row_delta[:, first:])).astype(jnp.bfloat16))
    dq_t = joined(
        jnp.add, [dot(key_t[:, i : i + band], part) for i, part in zip(starts, grads)]
    )
    dq = dq_t.T * scaling
    for first in starts:
        send(0, first, dq[first : first + band])
    for first, part in zip(starts, grads):
        send(1, first, dot(part, query[first:]) * scaling)
    for copy in copies:
        copy.wait()


def attention(packed, gain, band):
    shards, rows, width = packed.shape
    slots = (rows - EXTRA) // 4
    total = shards * slots
    vmem = pl.BlockSpec(memory_space=pltpu.VMEM)
    return pl.pallas_call(
        functools.partial(attention_kernel, band),
        in_specs=[vmem, vmem],
        out_specs=[pl.BlockSpec(memory_space=pl.ANY), vmem],
        out_shape=[
            jax.ShapeDtypeStruct((shards, 3 * slots, width), jnp.bfloat16),
            jax.ShapeDtypeStruct((1, width), jnp.float32),
        ],
        scratch_shapes=[
            pltpu.VMEM((total, width), jnp.bfloat16),
            pltpu.VMEM((total, width), jnp.bfloat16),
            pltpu.VMEM((total, width), jnp.float32),
            pltpu.VMEM((shards, 3 * slots, width), jnp.bfloat16),
            pltpu.SemaphoreType.DMA((total // band, 3)),
        ],
        compiler_params=pltpu.CompilerParams(vmem_limit_bytes=40 * 2**20),
        name="attention_grads",
    )(packed, gain)


def unpack_kernel(
    grads_ref, here_ref, other_ref, dq_ref, dk_ref, dv_ref, gain_ref, staged_ref, sum_ref, sems
):
    slots = dq_ref.shape[1]
    sum_ref[...] = here_ref[...] + other_ref[...]
    copies = [pltpu.make_async_copy(sum_ref, gain_ref, sems.at[3])]
    copies[0].start()
    for kind, out_ref in enumerate((dq_ref, dk_ref, dv_ref)):
        for head in range(grads_ref.shape[0]):
            cols = slice(head * HD, (head + 1) * HD)
            rows = slice(kind * slots, (kind + 1) * slots)
            staged_ref[kind, 0, :, cols] = grads_ref[head, rows, :]
        copy = pltpu.make_async_copy(staged_ref.at[kind], out_ref, sems.at[kind])
        copy.start()
        copies.append(copy)
    for copy in copies:
        copy.wait()


def unpack(grads, here, other):
    heads, rows, width = grads.shape
    shape = (1, rows // 3, heads * width)
    vmem = pl.BlockSpec(memory_space=pltpu.VMEM)
    return pl.pallas_call(
        unpack_kernel,
        in_specs=[vmem] * 3,
        out_specs=[pl.BlockSpec(memory_space=pl.ANY)] * 4,
        out_shape=[jax.ShapeDtypeStruct(shape, jnp.bfloat16)] * 3
        + [jax.ShapeDtypeStruct((1, width), jnp.float32)],
        scratch_shapes=[
            pltpu.VMEM((3,) + shape, jnp.bfloat16),
            pltpu.VMEM((1, width), jnp.float32),
            pltpu.SemaphoreType.DMA((4,)),
        ],
        compiler_params=pltpu.CompilerParams(vmem_limit_bytes=16 * 2**20),
        name="unpack_grads",
    )(grads, here, other)


RING_STEPS = (1, 7, 2)


def group_half(value, mask):
    count = lax.axis_size("grp")
    return lax.ppermute(value, "grp", [(i, i ^ mask) for i in range(count)])


def per_device(queries, attn_keys, attn_values, byte_grads, seg_starts, up_gain):
    packed = pack(queries, attn_keys, attn_values, byte_grads, seg_starts, 2)
    received = lax.all_to_all(packed, "seq", split_axis=0, concat_axis=0, tiled=True)
    gain = lax.dynamic_slice_in_dim(up_gain.reshape(-1, HD), lax.axis_index("seq"), 1)
    grads, gain_grad = attention(received, gain, 256)
    returned = lax.all_to_all(grads, "seq", split_axis=0, concat_axis=0, tiled=True)
    for mask in RING_STEPS[:-1]:
        gain_grad = gain_grad + group_half(gain_grad, mask)
    other = group_half(gain_grad, RING_STEPS[-1])
    dq, dk, dv, gain_grad = unpack(returned, gain_grad, other)
    return dq, dk, dv, gain_grad.reshape(HD)


def solution(mesh):
    rows = P("grp", "seq", None)
    return jax.shard_map(
        per_device,
        mesh=mesh,
        in_specs=(rows, rows, rows, rows, rows, P()),
        out_specs=(rows, rows, rows, P("seq")),
        check_vma=False,
    )
```

```python
import functools
import math

import jax
import jax.numpy as jnp
from jax import lax
from jax.experimental import pallas as pl
from jax.experimental.pallas import tpu as pltpu
from jax.sharding import PartitionSpec as P

HD = 128
EXTRA = 8


def start_columns(starts, byte_count):
    count = starts.shape[1]
    row = lax.broadcasted_iota(jnp.int32, (count, count), 0)
    col = lax.broadcasted_iota(jnp.int32, (count, count), 1)
    spread = jnp.broadcast_to(starts, (count, count))
    begin = jnp.sum(jnp.where(row == col, spread, 0), axis=1, keepdims=True)
    end = jnp.sum(jnp.where(row + 1 == col, spread, 0), axis=1, keepdims=True)
    last_row = lax.broadcasted_iota(jnp.int32, (count, 1), 0) == count - 1
    return begin, jnp.where(last_row, byte_count, end)


def pack_kernel(query_ref, key_ref, value_ref, bytes_ref, starts_ref, packed_ref):
    heads = packed_ref.shape[0]
    slots = query_ref.shape[1]
    byte_count = bytes_ref.shape[1]
    starts = starts_ref[0].astype(jnp.float32)
    begin, end = start_columns(starts, float(byte_count))
    position = lax.broadcasted_iota(jnp.int32, (slots, byte_count), 1).astype(jnp.float32)
    own = (begin <= position) & (position < end)
    filled = jnp.sum(jnp.where(starts < byte_count, 1.0, 0.0), axis=1, keepdims=True)
    first = jnp.min(starts, axis=1, keepdims=True)
    last = jnp.max(jnp.where(starts < byte_count, starts, -1.0), axis=1, keepdims=True)
    row = lax.broadcasted_iota(jnp.int32, (EXTRA, byte_count), 0)
    place = lax.broadcasted_iota(jnp.int32, (EXTRA, byte_count), 1).astype(jnp.float32)
    leading = (row < 2) & (place < first)
    tail = (row == 2) & (place >= last)
    member = jnp.concatenate(
        [jnp.where(own, 1.0, 0.0), jnp.where(leading | tail, 1.0, 0.0)], axis=0
    ).astype(jnp.bfloat16)
    sums = jnp.dot(member, bytes_ref[0], preferred_element_type=jnp.float32)
    extra = sums[slots:]
    low = extra - extra.astype(jnp.bfloat16).astype(jnp.float32)
    kind = lax.broadcasted_iota(jnp.int32, extra.shape, 0)
    extra = jnp.where(kind == 0, extra, jnp.where(kind == 3, filled, low)).astype(jnp.bfloat16)
    pooled = sums[:slots].astype(jnp.bfloat16)
    for head in range(heads):
        cols = slice(head * HD, (head + 1) * HD)
        packed_ref[head, 0:slots, :] = query_ref[0, :, cols]
        packed_ref[head, slots : 2 * slots, :] = key_ref[0, :, cols]
        packed_ref[head, 2 * slots : 3 * slots, :] = value_ref[0, :, cols]
        packed_ref[head, 3 * slots : 4 * slots, :] = pooled[:, cols]
        packed_ref[head, 4 * slots :, :] = extra[:, cols]


def pack(queries, attn_keys, attn_values, byte_grads, seg_starts, steps):
    slots, width = queries.shape[1:]
    byte_count = byte_grads.shape[1]
    cap = seg_starts.shape[2]
    cols = width // steps
    heads = width // HD
    rows = 4 * slots + EXTRA
    slot_spec = pl.BlockSpec((1, slots, cols), lambda i: (0, 0, i))
    return pl.pallas_call(
        pack_kernel,
        grid=(steps,),
        in_specs=[
            slot_spec,
            slot_spec,
            slot_spec,
            pl.BlockSpec((1, byte_count, cols), lambda i: (0, 0, i)),
            pl.BlockSpec((1, 1, cap), lambda i: (0, 0, 0)),
        ],
        out_specs=pl.BlockSpec((heads // steps, rows, HD), lambda i: (i, 0, 0)),
        out_shape=jax.ShapeDtypeStruct((heads, rows, HD), jnp.bfloat16),
        compiler_params=pltpu.CompilerParams(vmem_limit_bytes=60 * 2**20),
        name="pool_and_pack",
    )(queries, attn_keys, attn_values, byte_grads, seg_starts)


def dot(left, right):
    return jnp.dot(left, right, preferred_element_type=jnp.float32)


def dot_t(left, right):
    contract_last = (((1,), (1,)), ((), ()))
    return lax.dot_general(left, right, contract_last, preferred_element_type=jnp.float32)


def joined(combine, parts):
    whole = parts[0]
    for part in parts[1:]:
        first = whole.shape[1] - part.shape[1]
        whole = jnp.concatenate([whole[:, :first], combine(whole[:, first:], part)], axis=1)
    return whole


def attention_kernel(
    band,
    packed_ref,
    gain_ref,
    grads_ref,
    gain_grad_ref,
    upstream_ref,
    pooled_ref,
    bias_ref,
    staged_ref,
    sems,
):
    shards, rows, width = packed_ref.shape
    slots = (rows - EXTRA) // 4
    total = shards * slots
    scaling = 1.0 / math.sqrt(width)

    extra = packed_ref[:, 4 * slots :, :].astype(jnp.float32)
    carried = extra[:, 0:1, :] + extra[:, 1:2, :]
    incoming = jnp.concatenate([carried[1:], jnp.zeros_like(carried[:1])], axis=0)
    incoming = incoming + extra[:, 2:3, :]
    filled = extra[:, 3:4, :]
    slot = lax.broadcasted_iota(jnp.int32, (shards, slots, width), 1).astype(jnp.float32)
    pooled = packed_ref[:, 3 * slots : 4 * slots, :].astype(jnp.float32)
    pooled = pooled + jnp.where(slot == filled - 1.0, incoming, 0.0)
    pooled = pooled.reshape(total, width).astype(jnp.bfloat16)
    pooled_ref[...] = pooled
    upstream_ref[...] = (gain_ref[...] * pooled.astype(jnp.float32)).astype(jnp.bfloat16)
    bias_ref[...] = jnp.where(slot < filled, 0.0, -1e30).reshape(total, width)

    query = packed_ref[:, 0:slots, :].reshape(total, width)
    key = packed_ref[:, slots : 2 * slots, :].reshape(total, width)
    value = packed_ref[:, 2 * slots : 3 * slots, :].reshape(total, width)
    key_t = key.T
    value_t = value.T
    causal = lax.broadcasted_iota(jnp.int32, (band, band), 0) <= lax.broadcasted_iota(
        jnp.int32, (band, band), 1
    )
    upstream = upstream_ref[...]
    starts = range(0, total, band)
    copies = []

    def send(kind, first, array):
        owners = slice(first // slots, (first + band) // slots)
        rows = slice(kind * slots, (kind + 1) * slots)
        staged_ref[owners, rows, :] = array.astype(jnp.bfloat16).reshape(-1, slots, width)
        copy = pltpu.make_async_copy(
            staged_ref.at[owners, rows], grads_ref.at[owners, rows], sems.at[first // band, kind]
        )
        copy.start()
        copies.append(copy)

    scores = []
    for first in starts:
        part = dot_t(key[first : first + band], query[first:])
        bias = bias_ref[first : first + band]
        part = part + jnp.concatenate([bias] * ((total - first) // width), axis=1)
        square = jnp.where(causal, part[:, :band], -1e30)
        if first + band < total:
            square = jnp.concatenate([square, part[:, band:]], axis=1)
        scores.append(square)
    grad_probs = [dot_t(value[i : i + band], upstream[i:]) for i in starts]
    row_max = joined(jnp.maximum, [jnp.max(part, axis=0, keepdims=True) for part in scores])
    weights = [
        jnp.exp((part - row_max[:, first:]) * scaling) for first, part in zip(starts, scores)
    ]
    inverse = 1.0 / joined(jnp.add, [jnp.sum(part, axis=0, keepdims=True) for part in weights])
    probs = [part * inverse[:, first:] for first, part in zip(starts, weights)]
    probs_low = [part.astype(jnp.bfloat16) for part in probs]
    out_t = joined(
        jnp.add,
        [dot(value_t[:, i : i + band], part) for i, part in zip(starts, probs_low)],
    )
    for first, part in zip(starts, probs_low):
        send(2, first, dot(part, upstream[first:]))
    out_t = out_t.astype(jnp.bfloat16).astype(jnp.float32)
    row_delta = jnp.sum(upstream.astype(jnp.float32).T * out_t, axis=0, keepdims=True)
    gain_grad_ref[...] = jnp.sum(
        out_t.T * pooled_ref[...].astype(jnp.float32), axis=0, keepdims=True
    )
    grads = []
    for first, part, grad in zip(starts, probs, grad_probs):
        grads.append((part * (grad - row_delta[:, first:])).astype(jnp.bfloat16))
    dq_t = joined(
        jnp.add, [dot(key_t[:, i : i + band], part) for i, part in zip(starts, grads)]
    )
    dq = dq_t.T * scaling
    for first in starts:
        send(0, first, dq[first : first + band])
    for first, part in zip(starts, grads):
        send(1, first, dot(part, query[first:]) * scaling)
    for copy in copies:
        copy.wait()


def attention(packed, gain, band):
    shards, rows, width = packed.shape
    slots = (rows - EXTRA) // 4
    total = shards * slots
    vmem = pl.BlockSpec(memory_space=pltpu.VMEM)
    return pl.pallas_call(
        functools.partial(attention_kernel, band),
        in_specs=[vmem, vmem],
        out_specs=[pl.BlockSpec(memory_space=pl.ANY), vmem],
        out_shape=[
            jax.ShapeDtypeStruct((shards, 3 * slots, width), jnp.bfloat16),
            jax.ShapeDtypeStruct((1, width), jnp.float32),
        ],
        scratch_shapes=[
            pltpu.VMEM((total, width), jnp.bfloat16),
            pltpu.VMEM((total, width), jnp.bfloat16),
            pltpu.VMEM((total, width), jnp.float32),
            pltpu.VMEM((shards, 3 * slots, width), jnp.bfloat16),
            pltpu.SemaphoreType.DMA((total // band, 3)),
        ],
        compiler_params=pltpu.CompilerParams(vmem_limit_bytes=40 * 2**20),
        name="attention_grads",
    )(packed, gain)


def unpack_kernel(
    grads_ref, here_ref, other_ref, dq_ref, dk_ref, dv_ref, gain_ref, staged_ref, sum_ref, sems
):
    slots = dq_ref.shape[1]
    sum_ref[...] = here_ref[...] + other_ref[...]
    copies = [pltpu.make_async_copy(sum_ref, gain_ref, sems.at[3])]
    copies[0].start()
    for kind, out_ref in enumerate((dq_ref, dk_ref, dv_ref)):
        for head in range(grads_ref.shape[0]):
            cols = slice(head * HD, (head + 1) * HD)
            rows = slice(kind * slots, (kind + 1) * slots)
            staged_ref[kind, 0, :, cols] = grads_ref[head, rows, :]
        copy = pltpu.make_async_copy(staged_ref.at[kind], out_ref, sems.at[kind])
        copy.start()
        copies.append(copy)
    for copy in copies:
        copy.wait()


def unpack(grads, here, other):
    heads, rows, width = grads.shape
    shape = (1, rows // 3, heads * width)
    vmem = pl.BlockSpec(memory_space=pltpu.VMEM)
    return pl.pallas_call(
        unpack_kernel,
        in_specs=[vmem] * 3,
        out_specs=[pl.BlockSpec(memory_space=pl.ANY)] * 4,
        out_shape=[jax.ShapeDtypeStruct(shape, jnp.bfloat16)] * 3
        + [jax.ShapeDtypeStruct((1, width), jnp.float32)],
        scratch_shapes=[
            pltpu.VMEM((3,) + shape, jnp.bfloat16),
            pltpu.VMEM((1, width), jnp.float32),
            pltpu.SemaphoreType.DMA((4,)),
        ],
        compiler_params=pltpu.CompilerParams(vmem_limit_bytes=16 * 2**20),
        name="unpack_grads",
    )(grads, here, other)


RING_STEPS = (1, 7, 2)


def group_half(value, mask):
    count = lax.axis_size("grp")
    return lax.ppermute(value, "grp", [(i, i ^ mask) for i in range(count)])


def per_device(queries, attn_keys, attn_values, byte_grads, seg_starts, up_gain):
    packed = pack(queries, attn_keys, attn_values, byte_grads, seg_starts, 2)
    received = lax.all_to_all(packed, "seq", split_axis=0, concat_axis=0, tiled=True)
    gain = lax.dynamic_slice_in_dim(up_gain.reshape(-1, HD), lax.axis_index("seq"), 1)
    grads, gain_grad = attention(received, gain, 128)
    returned = lax.all_to_all(grads, "seq", split_axis=0, concat_axis=0, tiled=True)
    for mask in RING_STEPS[:-1]:
        gain_grad = gain_grad + group_half(gain_grad, mask)
    other = group_half(gain_grad, RING_STEPS[-1])
    dq, dk, dv, gain_grad = unpack(returned, gain_grad, other)
    return dq, dk, dv, gain_grad.reshape(HD)


def solution(mesh):
    rows = P("grp", "seq", None)
    return jax.shard_map(
        per_device,
        mesh=mesh,
        in_specs=(rows, rows, rows, rows, rows, P()),
        out_specs=(rows, rows, rows, P("seq")),
        check_vma=False,
    )
```
